32 devices in a mesh: wide: 4 (over y, core), narrow: 8 (over z, x).
Axes of the slice: x: 2, y: 2, z: 4, core: 2. Of those that a mesh axis runs over, the one named last changes fastest.
Arguments:
- leaf_rhs: bfloat16 [64, 1024, 256], P('wide', 'narrow'), may hold values from -6 to 6
- leaf_inv: bfloat16 [64, 256, 256], P('wide', 'narrow'), may hold values from -0.375 to 0.375
- leaf_upd: bfloat16 [64, 5, 256, 256], P('wide', None, 'narrow'), may hold values from -0.0390625 to 0.0390625
- leaf_targets: int32 [64, 5], P('wide'), may hold values from 0 to 2
- sep_rhs: bfloat16 [3, 1024, 256], P(None, 'narrow'), may hold values from -6 to 6
- sep_inv: bfloat16 [3, 256, 256], replicated, may hold values from -0.375 to 0.375
- sep_low: bfloat16 [3, 256, 256], replicated, may hold values from -0.21875 to 0.21875
Outputs:
- leaf_sol: bfloat16 [64, 1024, 256], P('wide', 'narrow')
- sep_sol: bfloat16 [3, 1024, 256], P(None, 'narrow')
The draws below stay inside these ranges and needn't reach their ends.
All inputs are finite; a program needn't handle non-finite values.
Results may differ from the reference program's by a relative error of at most 0.012.
Values may be sent and summed in bfloat16 or wider, within the bound.
A program may use at most 64 MiB of HBM per device.

```python
import jax
import jax.numpy as jnp
from jax import lax

B = 256
NUPD = 5
SEP = 3
NLEAF = 64
NRHS = 1024


def plant(entries, own_key, least, top_value):
    longest = entries.shape.index(max(entries.shape))
    spots = []
    for shift in (0, 1):
        where = [jax.random.randint(jax.random.fold_in(own_key, axis), (), 0, length) for axis, length in enumerate(entries.shape)]
        where[longest] = (where[longest] + shift) % entries.shape[longest]
        spots.append(tuple(where))
    return entries.at[spots[0]].set(least).at[spots[1]].set(top_value)


def steps_of(own_key, shape, pieces, low, largest):
    factor_of, own = 1.0, jax.random.fold_in(own_key, 6)
    for axis_at, shards_of in pieces:
        heights = jnp.exp(jax.random.uniform(jax.random.fold_in(own, axis_at), (shards_of,), jnp.float32, low / len(pieces), largest / len(pieces)))
        factor_of = factor_of * jnp.repeat(heights, shape[axis_at] // shards_of).reshape([-1 if axis == axis_at else 1 for axis in range(len(shape))])
    return factor_of


def scatter_about(stream_key, dims, deviation, limit, cuts=(), kind=jnp.bfloat16):
    level = steps_of(stream_key, dims, cuts, -0.22, 0.18) if cuts else 1.0
    result = jax.random.normal(stream_key, dims, jnp.float32) * deviation * level
    return jnp.minimum(jnp.maximum(result, -limit), limit).astype(kind)


def setup_inputs(seed: int = 0) -> dict:
    arg_keys = jax.random.split(jax.random.key(seed), 8)
    return {
        "leaf_rhs": scatter_about(arg_keys[0], (NLEAF, NRHS, B), 1.0, 6.0, ((0, 4), (1, 8))),
        "leaf_inv": scatter_about(arg_keys[1], (NLEAF, B, B), B ** -0.5, 0.375, ((0, 4), (1, 8))),
        "leaf_upd": scatter_about(arg_keys[2], (NLEAF, NUPD, B, B), (B * NLEAF * NUPD // SEP) ** -0.5, 0.0390625, ((0, 4), (2, 8))),
        "leaf_targets": plant(jax.random.randint(arg_keys[3], (NLEAF, NUPD), 0, SEP), jax.random.fold_in(arg_keys[3], 1), 0, SEP - 1).astype(jnp.int32),
        "sep_rhs": scatter_about(arg_keys[4], (SEP, NRHS, B), 1.0, 6.0, ((1, 8),)),
        "sep_inv": scatter_about(arg_keys[5], (SEP, B, B), B ** -0.5, 0.375),
        "sep_low": scatter_about(arg_keys[6], (SEP * (SEP - 1) // 2, B, B), (B * SEP) ** -0.5, 0.21875),
    }


def reference(leaf_rhs, leaf_inv, leaf_upd, leaf_targets, sep_rhs, sep_inv, sep_low):
    def step(total, item):
        rhs, inverse, blocks, targets = item
        solved = jnp.dot(rhs, inverse, preferred_element_type=jnp.float32).astype(jnp.bfloat16)
        onehot = (targets[:, None] == jnp.arange(SEP, dtype=jnp.int32)[None, :]).astype(jnp.float32)
        for block in range(NUPD):
            contrib = jnp.dot(solved, blocks[block], preferred_element_type=jnp.float32)
            total = total + onehot[block][:, None, None] * contrib[None]
        return total, solved

    start = jnp.zeros((SEP, NRHS, B), jnp.float32)
    gathered, leaf_sol = lax.scan(step, start, (leaf_rhs, leaf_inv, leaf_upd, leaf_targets))
    solved_list = []
    for row in range(SEP):
        reduced = sep_rhs[row].astype(jnp.float32) - gathered[row]
        for col in range(row):
            reduced = reduced - jnp.dot(solved_list[col], sep_low[row * (row - 1) // 2 + col], preferred_element_type=jnp.float32)
        reduced = reduced.astype(jnp.bfloat16)
        solved_list.append(jnp.dot(reduced, sep_inv[row], preferred_element_type=jnp.float32).astype(jnp.bfloat16))
    return leaf_sol, jnp.stack(solved_list)
```

```python
import functools

import jax
import jax.numpy as jnp
from jax import lax
from jax.experimental import pallas as pl
from jax.experimental.pallas import tpu as pltpu
from jax.sharding import PartitionSpec as P


def separator_solve(gathered, sep_rhs, sep_inv, sep_low):
    nsep = sep_inv.shape[0]
    solved_list = []
    for row in range(nsep):
        reduced = sep_rhs[row].astype(jnp.float32) - gathered[row]
        for col in range(row):
            reduced = reduced - jnp.dot(
                solved_list[col],
                sep_low[row * (row - 1) // 2 + col],
                preferred_element_type=jnp.float32,
            )
        reduced = reduced.astype(jnp.bfloat16)
        solved_list.append(
            jnp.dot(reduced, sep_inv[row], preferred_element_type=jnp.float32).astype(jnp.bfloat16)
        )
    return jnp.stack(solved_list)


def plain_body(leaf_rhs, leaf_inv, leaf_upd, leaf_targets, sep_rhs, sep_inv, sep_low):
    nsep = sep_inv.shape[0]
    nupd = leaf_upd.shape[1]
    leaves, scenarios, width = leaf_rhs.shape
    onehot = (leaf_targets[:, :, None] == jnp.arange(nsep, dtype=jnp.int32)[None, None, :]).astype(
        jnp.float32
    )
    columns = leaf_rhs
    leaf_sol = jnp.einsum(
        "lcj,lji->lci",
        columns,
        lax.all_gather(leaf_inv, "narrow", axis=1, tiled=True),
        preferred_element_type=jnp.float32,
    ).astype(jnp.bfloat16)
    start_sum = jnp.zeros((nsep, scenarios, width), jnp.float32)
    total = start_sum
    piece = lax.all_gather(leaf_upd, "narrow", axis=2, tiled=True)
    columns = leaf_sol
    for block in range(nupd):
        contrib = jnp.einsum(
            "lcj,lji->lci", columns, piece[:, block], preferred_element_type=jnp.float32
        )
        total = total + jnp.einsum("lci,ls->sci", contrib, onehot[:, block])
    gathered = total
    total = lax.psum(gathered, "wide")
    sep_sol = separator_solve(total, sep_rhs, sep_inv, sep_low)
    return (leaf_sol, sep_sol)


CHUNKS = 4
NX = 2
MESH = pl.DeviceIdType.MESH


def kernel(nz, rhs_ref, inv_ref, upd_ref, tgt_ref, srhs_ref, sinv_ref, slow_ref, sol_ref, sep_ref,
           inv_g, sol_s, sol_r, wf, wt, part, r1, q1, r2, q2, r3, gall,
           zs, zr, xs, xr, as_, ar, s1, v1, s2, v2, s3, v3, s4, v4):
    nn = nz * NX
    w, n = lax.axis_index("wide"), lax.axis_index("narrow")
    core, y = lax.rem(w, 2), w // 2
    z, x = n // NX, lax.rem(n, NX)
    leaves, rows, width = inv_ref.shape
    nupd = upd_ref.shape[1]
    scen = rhs_ref.shape[1]
    nsep = sinv_ref.shape[0]
    per = leaves // CHUNKS
    slab = nsep * width // 4

    barrier = pltpu.get_barrier_semaphore()
    for k in range(1, nn):
        pl.semaphore_signal(barrier, inc=1, device_id={"wide": w, "narrow": lax.rem(n + k, nn)}, device_id_type=MESH)
    for k in range(1, 4):
        pl.semaphore_signal(barrier, inc=1, device_id={"wide": lax.rem(w + k, 4), "narrow": n}, device_id_type=MESH)
    inv_g[n] = inv_ref[...]
    pl.semaphore_wait(barrier, nn - 1 + 3)

    def send(src, dst, ss, rs, wide, narrow):
        return pltpu.make_async_remote_copy(
            src_ref=src, dst_ref=dst, send_sem=ss, recv_sem=rs,
            device_id={"wide": wide, "narrow": narrow}, device_id_type=MESH)

    def z_copy(c, way, hop, block_z):
        step = 1 - 2 * way
        ref = inv_g.at[block_z * NX + x, pl.ds(c * per, per)]
        return send(ref, ref, zs.at[c, way, hop], zr.at[c, way, hop], w, (z + step) * NX + x)

    def x_copy(c, block_z, side):
        ref = inv_g.at[block_z * NX + side, pl.ds(c * per, per)]
        return send(ref, ref, xs.at[c, block_z], xr.at[c, block_z], w, z * NX + 1 - x)

    def can_send(way, hop):
        if way == 0:
            return jnp.logical_and(z - hop >= 0, z + 1 <= nz - 1)
        return jnp.logical_and(z + hop <= nz - 1, z - 1 >= 0)

    def source(way, hop):
        return z - hop if way == 0 else z + hop

    def has_recv(way, hop):
        return z - 1 - hop >= 0 if way == 0 else z + 1 + hop <= nz - 1

    for c in range(CHUNKS):
        for way in range(2):
            @pl.when(can_send(way, 0))
            def _(c=c, way=way):
                z_copy(c, way, 0, source(way, 0)).start()
        x_copy(c, z, x).start()

    for s in range(nsep):
        def combine(l, carry, s=s):
            acc = jnp.zeros((rows, width), jnp.float32)
            for u in range(nupd):
                pick = jnp.where(tgt_ref[l, u] == s, 1.0, 0.0).astype(jnp.float32)
                acc = acc + pick * upd_ref[l, u].astype(jnp.float32)
            wf[l] = acc
            return carry
        lax.fori_loop(0, leaves, combine, 0)
        wt[pl.ds(s * width, width), :] = wf[...].reshape(leaves * rows, width).T.astype(jnp.bfloat16)

    def relay(c):
        for hop in range(nz - 1):
            for way in range(2):
                @pl.when(has_recv(way, hop))
                def _(hop=hop, way=way):
                    step = 1 - 2 * way
                    block_z = source(way, hop + 1)
                    ref = inv_g.at[block_z * NX + x, pl.ds(c * per, per)]
                    send(ref, ref, zs.at[c, way, hop], zr.at[c, way, hop], w, (z - step) * NX + x).wait_recv()
                    x_copy(c, block_z, x).start()
                    if hop + 1 < nz - 1:
                        @pl.when(can_send(way, hop + 1))
                        def _():
                            z_copy(c, way, hop + 1, block_z).start()

    def a_copy(c, peer, owner, sem):
        return send(sol_s.at[peer, pl.ds(c * per, per)], sol_r.at[owner, pl.ds(c * per, per)],
                    as_.at[c, sem], ar.at[c, sem], w, peer)

    def solve(c):
        for b in range(nz):
            x_copy(c, b, 1 - x).wait_recv()

        def one(i, carry):
            l = c * per + i
            full = inv_g[:, l].reshape(nn * rows, width)
            out = jnp.dot(rhs_ref[l], full, preferred_element_type=jnp.float32)
            sol_ref[l] = out.astype(jnp.bfloat16)
            sol_s[:, l] = out.T.astype(jnp.bfloat16).reshape(nn, rows, scen)
            return carry
        lax.fori_loop(0, per, one, 0)
        for k in range(1, nn):
            a_copy(c, lax.rem(n + k, nn), n, k).start()

    relay(0)
    for c in range(CHUNKS):
        if c + 1 < CHUNKS:
            relay(c + 1)
        solve(c)
    sol_r[n] = sol_s[n]

    mate, across = w + 1 - 2 * core, lax.rem(w + 2, 4)

    def c1(m, k):
        return send(part.at[m, 1 - core], r1.at[m], s1.at[k], v1.at[k], mate, n)

    def c2(m, k):
        return send(q1.at[m, 1 - y], r2.at[m], s2.at[k], v2.at[k], across, n)

    def c3(m, k):
        return send(q2.at[m], r3.at[n], s3.at[k], v3.at[k], w, m)

    def multiply(k):
        m = lax.rem(n + nn - k, nn)
        if k:
            for c in range(CHUNKS):
                a_copy(c, m, m, k).wait_recv()
        block = sol_r[m].reshape(leaves * rows, scen)
        out = jnp.dot(wt[...], block, preferred_element_type=jnp.float32).astype(jnp.bfloat16)
        for a in range(2):
            for b in range(2):
                q = b * 2 + a
                part[m, a, b] = out[q * slab:(q + 1) * slab]
        c1(m, k).start()

    def add_core(k):
        m = lax.rem(n + nn - k, nn)
        c1(m, k).wait_recv()
        q1[m] = (part[m, core].astype(jnp.float32) + r1[m].astype(jnp.float32)).astype(jnp.bfloat16)
        c2(m, k).start()

    def add_across(k):
        m = lax.rem(n + nn - k, nn)
        c2(m, k).wait_recv()
        q2[m] = (q1[m, y].astype(jnp.float32) + r2[m].astype(jnp.float32)).astype(jnp.bfloat16)
        if k:
            c3(m, k).start()

    order = list(range(1, nn)) + [0]
    for i in range(nn + 2):
        if i < nn:
            multiply(order[i])
        if 0 <= i - 1 < nn:
            add_core(order[i - 1])
        if 0 <= i - 2 < nn:
            add_across(order[i - 2])

    total = q2[n].astype(jnp.float32)
    for k in range(1, nn):
        m = lax.rem(n + k, nn)
        send(q2.at[m], r3.at[m], s3.at[k], v3.at[k], w, m).wait_recv()
        total = total + r3[m].astype(jnp.float32)
    gall[w] = total.astype(jnp.bfloat16)
    for k in range(1, 4):
        send(gall.at[w], gall.at[w], s4.at[k], v4.at[k], lax.rem(w + k, 4), n).start()
    for k in range(1, 4):
        m = lax.rem(w + 4 - k, 4)
        send(gall.at[m], gall.at[m], s4.at[k], v4.at[k], m, n).wait_recv()
    gathered = gall[...].astype(jnp.float32).reshape(nsep * width, scen)
    solved = []
    for s in range(nsep):
        reduced = srhs_ref[s].astype(jnp.float32) - gathered[s * width:(s + 1) * width].T
        for t in range(s):
            reduced = reduced - jnp.dot(solved[t], slow_ref[s * (s - 1) // 2 + t], preferred_element_type=jnp.float32)
        solved.append(jnp.dot(reduced.astype(jnp.bfloat16), sinv_ref[s], preferred_element_type=jnp.float32).astype(jnp.bfloat16))
        sep_ref[s] = solved[s]

    for c in range(CHUNKS):
        for way in range(2):
            for hop in range(nz - 1):
                @pl.when(can_send(way, hop))
                def _(c=c, way=way, hop=hop):
                    z_copy(c, way, hop, source(way, hop)).wait_send()
        for b in range(nz):
            x_copy(c, b, x).wait_send()
        for k in range(1, nn):
            a_copy(c, lax.rem(n + k, nn), n, k).wait_send()
    for k in range(nn):
        m = lax.rem(n + nn - k, nn)
        c1(m, k).wait_send()
        c2(m, k).wait_send()
        if k:
            c3(m, k).wait_send()
    for k in range(1, 4):
        send(gall.at[w], gall.at[w], s4.at[k], v4.at[k], lax.rem(w + k, 4), n).wait_send()


def fused_body(nn, leaf_rhs, leaf_inv, leaf_upd, leaf_targets, sep_rhs, sep_inv, sep_low):
    leaves, scen, width = leaf_rhs.shape
    rows = leaf_inv.shape[1]
    nsep = sep_inv.shape[0]
    nz = nn // NX
    slab = nsep * width // 4
    bf = jnp.bfloat16
    vmem = pl.BlockSpec(memory_space=pltpu.VMEM)
    dma = pltpu.SemaphoreType.DMA
    return pl.pallas_call(
        functools.partial(kernel, nz),
        out_shape=(jax.ShapeDtypeStruct(leaf_rhs.shape, bf), jax.ShapeDtypeStruct(sep_rhs.shape, bf)),
        in_specs=[vmem, vmem, vmem, pl.BlockSpec(memory_space=pltpu.SMEM), vmem, vmem, vmem],
        out_specs=(vmem, vmem),
        scratch_shapes=[
            pltpu.VMEM((nn, leaves, rows, width), bf),
            pltpu.VMEM((nn, leaves, rows, scen), bf),
            pltpu.VMEM((nn, leaves, rows, scen), bf),
            pltpu.VMEM((leaves, rows, width), jnp.float32),
            pltpu.VMEM((nsep * width, leaves * rows), bf),
            pltpu.VMEM((nn, 2, 2, slab, scen), bf),
            pltpu.VMEM((nn, 2, slab, scen), bf),
            pltpu.VMEM((nn, 2, slab, scen), bf),
            pltpu.VMEM((nn, slab, scen), bf),
            pltpu.VMEM((nn, slab, scen), bf),
            pltpu.VMEM((nn, slab, scen), bf),
            pltpu.VMEM((4, slab, scen), bf),
            dma((CHUNKS, 2, nz)), dma((CHUNKS, 2, nz)),
            dma((CHUNKS, nz)), dma((CHUNKS, nz)),
            dma((CHUNKS, nn)), dma((CHUNKS, nn)),
            dma((nn,)), dma((nn,)), dma((nn,)), dma((nn,)), dma((nn,)), dma((nn,)),
            dma((4,)), dma((4,)),
        ],
        compiler_params=pltpu.CompilerParams(
            collective_id=0, has_side_effects=True, vmem_limit_bytes=40 * 2**20),
    )(leaf_rhs, leaf_inv, leaf_upd, leaf_targets, sep_rhs, sep_inv, sep_low)


def solution(mesh):
    if mesh.shape["wide"] == 4 and mesh.shape["narrow"] == 8:
        body = functools.partial(fused_body, mesh.shape["narrow"])
    else:
        body = plain_body
    in_specs = (
        P("wide", "narrow", None),
        P("wide", "narrow", None),
        P("wide", None, "narrow", None),
        P("wide", None),
        P(None, "narrow", None),
        P(),
        P(),
    )
    out_specs = (P("wide", "narrow", None), P(None, "narrow", None))
    return jax.shard_map(body, mesh=mesh, in_specs=in_specs, out_specs=out_specs, check_vma=False)
```

```python
import functools

import jax
import jax.numpy as jnp
from jax import lax
from jax.experimental import pallas as pl
from jax.experimental.pallas import tpu as pltpu
from jax.sharding import PartitionSpec as P


def separator_solve(gathered, sep_rhs, sep_inv, sep_low):
    nsep = sep_inv.shape[0]
    solved_list = []
    for row in range(nsep):
        reduced = sep_rhs[row].astype(jnp.float32) - gathered[row]
        for col in range(row):
            reduced = reduced - jnp.dot(
                solved_list[col],
                sep_low[row * (row - 1) // 2 + col],
                preferred_element_type=jnp.float32,
            )
        reduced = reduced.astype(jnp.bfloat16)
        solved_list.append(
            jnp.dot(reduced, sep_inv[row], preferred_element_type=jnp.float32).astype(jnp.bfloat16)
        )
    return jnp.stack(solved_list)


def plain_body(leaf_rhs, leaf_inv, leaf_upd, leaf_targets, sep_rhs, sep_inv, sep_low):
    nsep = sep_inv.shape[0]
    nupd = leaf_upd.shape[1]
    leaves, scenarios, width = leaf_rhs.shape
    onehot = (leaf_targets[:, :, None] == jnp.arange(nsep, dtype=jnp.int32)[None, None, :]).astype(
        jnp.float32
    )
    columns = leaf_rhs
    leaf_sol = jnp.einsum(
        "lcj,lji->lci",
        columns,
        lax.all_gather(leaf_inv, "narrow", axis=1, tiled=True),
        preferred_element_type=jnp.float32,
    ).astype(jnp.bfloat16)
    start_sum = jnp.zeros((nsep, scenarios, width), jnp.float32)
    total = start_sum
    piece = lax.all_gather(leaf_upd, "narrow", axis=2, tiled=True)
    columns = leaf_sol
    for block in range(nupd):
        contrib = jnp.einsum(
            "lcj,lji->lci", columns, piece[:, block], preferred_element_type=jnp.float32
        )
        total = total + jnp.einsum("lci,ls->sci", contrib, onehot[:, block])
    gathered = total
    total = lax.psum(gathered, "wide")
    sep_sol = separator_solve(total, sep_rhs, sep_inv, sep_low)
    return (leaf_sol, sep_sol)


CHUNKS = 4
NX = 2
MESH = pl.DeviceIdType.MESH


def kernel(nz, rhs_hbm, inv_ref, upd_hbm, tgt_ref, srhs_hbm, sinv_hbm, slow_hbm, sol_ref, sep_ref,
           rhs_ref, upd_ref, srhs_ref, sinv_ref, slow_ref, load, inv_g, sol_s, sol_r, wf, wt, part, r1, q1, r2, q2, r3, gall,
           zs, zr, xs, xr, as_, ar, s1, v1, s2, v2, s3, v3, s4, v4):
    nn = nz * NX
    w, n = lax.axis_index("wide"), lax.axis_index("narrow")
    core, y = lax.rem(w, 2), w // 2
    z, x = n // NX, lax.rem(n, NX)
    leaves, rows, width = inv_ref.shape
    nupd = upd_hbm.shape[1]
    scen = rhs_hbm.shape[1]
    nsep = sinv_hbm.shape[0]
    per = leaves // CHUNKS
    slab = nsep * width // 4

    loads = [
        pltpu.make_async_copy(src, dst, load.at[i])
        for i, (src, dst) in enumerate([
            (inv_ref, inv_g.at[n]), (upd_hbm, upd_ref), (rhs_hbm, rhs_ref),
            (srhs_hbm, srhs_ref), (sinv_hbm, sinv_ref), (slow_hbm, slow_ref)])
    ]
    loads[0].start()
    barrier = pltpu.get_barrier_semaphore()
    for k in range(1, nn):
        pl.semaphore_signal(barrier, inc=1, device_id={"wide": w, "narrow": lax.rem(n + k, nn)}, device_id_type=MESH)
    for k in range(1, 4):
        pl.semaphore_signal(barrier, inc=1, device_id={"wide": lax.rem(w + k, 4), "narrow": n}, device_id_type=MESH)
    for copy in loads[1:]:
        copy.start()
    loads[0].wait()
    pl.semaphore_wait(barrier, nn - 1 + 3)

    def send(src, dst, ss, rs, wide, narrow):
        return pltpu.make_async_remote_copy(
            src_ref=src, dst_ref=dst, send_sem=ss, recv_sem=rs,
            device_id={"wide": wide, "narrow": narrow}, device_id_type=MESH)

    def z_copy(c, way, hop, block_z):
        step = 1 - 2 * way
        ref = inv_g.at[block_z * NX + x, pl.ds(c * per, per)]
        return send(ref, ref, zs.at[c, way, hop], zr.at[c, way, hop], w, (z + step) * NX + x)

    def x_copy(c, block_z, side):
        ref = inv_g.at[block_z * NX + side, pl.ds(c * per, per)]
        return send(ref, ref, xs.at[c, block_z], xr.at[c, block_z], w, z * NX + 1 - x)

    def can_send(way, hop):
        if way == 0:
            return jnp.logical_and(z - hop >= 0, z + 1 <= nz - 1)
        return jnp.logical_and(z + hop <= nz - 1, z - 1 >= 0)

    def source(way, hop):
        return z - hop if way == 0 else z + hop

    def has_recv(way, hop):
        return z - 1 - hop >= 0 if way == 0 else z + 1 + hop <= nz - 1

    for c in range(CHUNKS):
        for way in range(2):
            @pl.when(can_send(way, 0))
            def _(c=c, way=way):
                z_copy(c, way, 0, source(way, 0)).start()
        x_copy(c, z, x).start()

    loads[1].wait()
    for s in range(nsep):
        def combine(l, carry, s=s):
            acc = jnp.zeros((rows, width), jnp.float32)
            for u in range(nupd):
                pick = jnp.where(tgt_ref[u, l] == s, 1.0, 0.0).astype(jnp.float32)
                acc = acc + pick * upd_ref[l, u].astype(jnp.float32)
            wf[l] = acc
            return carry
        lax.fori_loop(0, leaves, combine, 0)
        wt[pl.ds(s * width, width), :] = wf[...].reshape(leaves * rows, width).T.astype(jnp.bfloat16)

    def relay(c):
        for hop in range(nz - 1):
            for way in range(2):
                @pl.when(has_recv(way, hop))
                def _(hop=hop, way=way):
                    step = 1 - 2 * way
                    block_z = source(way, hop + 1)
                    ref = inv_g.at[block_z * NX + x, pl.ds(c * per, per)]
                    send(ref, ref, zs.at[c, way, hop], zr.at[c, way, hop], w, (z - step) * NX + x).wait_recv()
                    x_copy(c, block_z, x).start()
                    if hop + 1 < nz - 1:
                        @pl.when(can_send(way, hop + 1))
                        def _():
                            z_copy(c, way, hop + 1, block_z).start()

    def a_copy(c, peer, owner, sem):
        return send(sol_s.at[peer, pl.ds(c * per, per)], sol_r.at[owner, pl.ds(c * per, per)],
                    as_.at[c, sem], ar.at[c, sem], w, peer)

    def solve(c):
        for b in range(nz):
            x_copy(c, b, 1 - x).wait_recv()

        def one(i, carry):
            l = c * per + i
            full = inv_g[:, l].reshape(nn * rows, width)
            out = jnp.dot(rhs_ref[l], full, preferred_element_type=jnp.float32)
            sol_ref[l] = out.astype(jnp.bfloat16)
            sol_s[:, l] = out.T.astype(jnp.bfloat16).reshape(nn, rows, scen)
            return carry
        lax.fori_loop(0, per, one, 0)
        for k in range(1, nn):
            a_copy(c, lax.rem(n + k, nn), n, k).start()

    loads[2].wait()
    relay(0)
    for c in range(CHUNKS):
        if c + 1 < CHUNKS:
            relay(c + 1)
        solve(c)
    sol_r[n] = sol_s[n]

    mate, across = w + 1 - 2 * core, lax.rem(w + 2, 4)

    def c1(m, k):
        return send(part.at[m, 1 - core], r1.at[m], s1.at[k], v1.at[k], mate, n)

    def c2(m, k):
        return send(q1.at[m, 1 - y], r2.at[m], s2.at[k], v2.at[k], across, n)

    def c3(m, k):
        return send(q2.at[m], r3.at[n], s3.at[k], v3.at[k], w, m)

    def multiply(k):
        m = lax.rem(n + nn - k, nn)
        if k:
            for c in range(CHUNKS):
                a_copy(c, m, m, k).wait_recv()
        block = sol_r[m].reshape(leaves * rows, scen)
        out = jnp.dot(wt[...], block, preferred_element_type=jnp.float32).astype(jnp.bfloat16)
        for a in range(2):
            for b in range(2):
                q = b * 2 + a
                part[m, a, b] = out[q * slab:(q + 1) * slab]
        c1(m, k).start()

    def add_core(k):
        m = lax.rem(n + nn - k, nn)
        c1(m, k).wait_recv()
        q1[m] = (part[m, core].astype(jnp.float32) + r1[m].astype(jnp.float32)).astype(jnp.bfloat16)
        c2(m, k).start()

    def add_across(k):
        m = lax.rem(n + nn - k, nn)
        c2(m, k).wait_recv()
        q2[m] = (q1[m, y].astype(jnp.float32) + r2[m].astype(jnp.float32)).astype(jnp.bfloat16)
        if k:
            c3(m, k).start()

    order = list(range(nn))
    for i in range(nn + 2):
        if i < nn:
            multiply(order[i])
        if 0 <= i - 1 < nn:
            add_core(order[i - 1])
        if 0 <= i - 2 < nn:
            add_across(order[i - 2])

    total = q2[n].astype(jnp.float32)
    for k in range(1, nn):
        m = lax.rem(n + k, nn)
        send(q2.at[m], r3.at[m], s3.at[k], v3.at[k], w, m).wait_recv()
        total = total + r3[m].astype(jnp.float32)
    gall[w] = total.astype(jnp.bfloat16)
    for k in range(1, 4):
        send(gall.at[w], gall.at[w], s4.at[k], v4.at[k], lax.rem(w + k, 4), n).start()
    for k in range(1, 4):
        m = lax.rem(w + 4 - k, 4)
        send(gall.at[m], gall.at[m], s4.at[k], v4.at[k], m, n).wait_recv()
    gathered = gall[...].astype(jnp.float32).reshape(nsep * width, scen)
    for copy in loads[3:]:
        copy.wait()
    solved = []
    for s in range(nsep):
        reduced = srhs_ref[s].astype(jnp.float32) - gathered[s * width:(s + 1) * width].T
        for t in range(s):
            reduced = reduced - jnp.dot(solved[t], slow_ref[s * (s - 1) // 2 + t], preferred_element_type=jnp.float32)
        solved.append(jnp.dot(reduced.astype(jnp.bfloat16), sinv_ref[s], preferred_element_type=jnp.float32).astype(jnp.bfloat16))
        sep_ref[s] = solved[s]

    for c in range(CHUNKS):
        for way in range(2):
            for hop in range(nz - 1):
                @pl.when(can_send(way, hop))
                def _(c=c, way=way, hop=hop):
                    z_copy(c, way, hop, source(way, hop)).wait_send()
        for b in range(nz):
            x_copy(c, b, x).wait_send()
        for k in range(1, nn):
            a_copy(c, lax.rem(n + k, nn), n, k).wait_send()
    for k in range(nn):
        m = lax.rem(n + nn - k, nn)
        c1(m, k).wait_send()
        c2(m, k).wait_send()
        if k:
            c3(m, k).wait_send()
    for k in range(1, 4):
        send(gall.at[w], gall.at[w], s4.at[k], v4.at[k], lax.rem(w + k, 4), n).wait_send()


def fused_body(nn, leaf_rhs, leaf_inv, leaf_upd, leaf_targets, sep_rhs, sep_inv, sep_low):
    leaves, scen, width = leaf_rhs.shape
    rows = leaf_inv.shape[1]
    nsep = sep_inv.shape[0]
    nz = nn // NX
    slab = nsep * width // 4
    bf = jnp.bfloat16
    vmem = pl.BlockSpec(memory_space=pltpu.VMEM)
    hbm = pl.BlockSpec(memory_space=pl.ANY)
    dma = pltpu.SemaphoreType.DMA
    return pl.pallas_call(
        functools.partial(kernel, nz),
        out_shape=(jax.ShapeDtypeStruct(leaf_rhs.shape, bf), jax.ShapeDtypeStruct(sep_rhs.shape, bf)),
        in_specs=[hbm, hbm, hbm, pl.BlockSpec(memory_space=pltpu.SMEM), hbm, hbm, hbm],
        out_specs=(vmem, vmem),
        scratch_shapes=[
            pltpu.VMEM(leaf_rhs.shape, bf), pltpu.VMEM(leaf_upd.shape, bf), pltpu.VMEM(sep_rhs.shape, bf),
            pltpu.VMEM(sep_inv.shape, bf), pltpu.VMEM(sep_low.shape, bf), dma((6,)),
            pltpu.VMEM((nn, leaves, rows, width), bf),
            pltpu.VMEM((nn, leaves, rows, scen), bf),
            pltpu.VMEM((nn, leaves, rows, scen), bf),
            pltpu.VMEM((leaves, rows, width), jnp.float32),
            pltpu.VMEM((nsep * width, leaves * rows), bf),
            pltpu.VMEM((nn, 2, 2, slab, scen), bf),
            pltpu.VMEM((nn, 2, slab, scen), bf),
            pltpu.VMEM((nn, 2, slab, scen), bf),
            pltpu.VMEM((nn, slab, scen), bf),
            pltpu.VMEM((nn, slab, scen), bf),
            pltpu.VMEM((nn, slab, scen), bf),
            pltpu.VMEM((4, slab, scen), bf),
            dma((CHUNKS, 2, nz)), dma((CHUNKS, 2, nz)),
            dma((CHUNKS, nz)), dma((CHUNKS, nz)),
            dma((CHUNKS, nn)), dma((CHUNKS, nn)),
            dma((nn,)), dma((nn,)), dma((nn,)), dma((nn,)), dma((nn,)), dma((nn,)),
            dma((4,)), dma((4,)),
        ],
        compiler_params=pltpu.CompilerParams(
            collective_id=0, has_side_effects=True, vmem_limit_bytes=56 * 2**20),
    )(leaf_rhs, leaf_inv, leaf_upd, leaf_targets.T, sep_rhs, sep_inv, sep_low)


def solution(mesh):
    if mesh.shape["wide"] == 4 and mesh.shape["narrow"] == 8:
        body = functools.partial(fused_body, mesh.shape["narrow"])
    else:
        body = plain_body
    in_specs = (
        P("wide", "narrow", None),
        P("wide", "narrow", None),
        P("wide", None, "narrow", None),
        P("wide", None),
        P(None, "narrow", None),
        P(),
        P(),
    )
    out_specs = (P("wide", "narrow", None), P(None, "narrow", None))
    return jax.shard_map(body, mesh=mesh, in_specs=in_specs, out_specs=out_specs, check_vma=False)
```

```python
import functools

import jax
import jax.numpy as jnp
from jax import lax
from jax.experimental import pallas as pl
from jax.experimental.pallas import tpu as pltpu
from jax.sharding import PartitionSpec as P


def separator_solve(gathered, sep_rhs, sep_inv, sep_low):
    nsep = sep_inv.shape[0]
    solved_list = []
    for row in range(nsep):
        reduced = sep_rhs[row].astype(jnp.float32) - gathered[row]
        for col in range(row):
            reduced = reduced - jnp.dot(
                solved_list[col],
                sep_low[row * (row - 1) // 2 + col],
                preferred_element_type=jnp.float32,
            )
        reduced = reduced.astype(jnp.bfloat16)
        solved_list.append(
            jnp.dot(reduced, sep_inv[row], preferred_element_type=jnp.float32).astype(jnp.bfloat16)
        )
    return jnp.stack(solved_list)


def plain_body(leaf_rhs, leaf_inv, leaf_upd, leaf_targets, sep_rhs, sep_inv, sep_low):
    nsep = sep_inv.shape[0]
    nupd = leaf_upd.shape[1]
    leaves, scenarios, width = leaf_rhs.shape
    onehot = (leaf_targets[:, :, None] == jnp.arange(nsep, dtype=jnp.int32)[None, None, :]).astype(
        jnp.float32
    )
    columns = leaf_rhs
    leaf_sol = jnp.einsum(
        "lcj,lji->lci",
        columns,
        lax.all_gather(leaf_inv, "narrow", axis=1, tiled=True),
        preferred_element_type=jnp.float32,
    ).astype(jnp.bfloat16)
    start_sum = jnp.zeros((nsep, scenarios, width), jnp.float32)
    total = start_sum
    piece = lax.all_gather(leaf_upd, "narrow", axis=2, tiled=True)
    columns = leaf_sol
    for block in range(nupd):
        contrib = jnp.einsum(
            "lcj,lji->lci", columns, piece[:, block], preferred_element_type=jnp.float32
        )
        total = total + jnp.einsum("lci,ls->sci", contrib, onehot[:, block])
    gathered = total
    total = lax.psum(gathered, "wide")
    sep_sol = separator_solve(total, sep_rhs, sep_inv, sep_low)
    return (leaf_sol, sep_sol)


CHUNKS = 4
NX = 2
MESH = pl.DeviceIdType.MESH


def kernel(nz, rhs_hbm, inv_ref, upd_hbm, tgt_ref, srhs_hbm, sinv_hbm, slow_hbm, sol_ref, sep_ref,
           rhs_ref, upd_ref, srhs_ref, sinv_ref, slow_ref, load, inv_g, sol_s, sol_r, wf, wt, part, r1, q1, r2, q2, r3, gall,
           zs, zr, xs, xr, as_, ar, s1, v1, s2, v2, s3, v3, s4, v4):
    nn = nz * NX
    w, n = lax.axis_index("wide"), lax.axis_index("narrow")
    core, y = lax.rem(w, 2), w // 2
    z, x = n // NX, lax.rem(n, NX)
    leaves, rows, width = inv_ref.shape
    nupd = upd_hbm.shape[1]
    scen = rhs_hbm.shape[1]
    nsep = sinv_hbm.shape[0]
    per = leaves // CHUNKS
    slab = nsep * width // 4

    loads = [
        pltpu.make_async_copy(src, dst, load.at[i])
        for i, (src, dst) in enumerate([
            (inv_ref, inv_g.at[n]), (upd_hbm, upd_ref), (rhs_hbm, rhs_ref),
            (srhs_hbm, srhs_ref), (sinv_hbm, sinv_ref), (slow_hbm, slow_ref)])
    ]
    loads[0].start()
    barrier = pltpu.get_barrier_semaphore()
    for k in range(1, nn):
        pl.semaphore_signal(barrier, inc=1, device_id={"wide": w, "narrow": lax.rem(n + k, nn)}, device_id_type=MESH)
    for k in range(1, 4):
        pl.semaphore_signal(barrier, inc=1, device_id={"wide": lax.rem(w + k, 4), "narrow": n}, device_id_type=MESH)
    for copy in loads[1:]:
        copy.start()
    loads[0].wait()
    pl.semaphore_wait(barrier, nn - 1 + 3)

    def send(src, dst, ss, rs, wide, narrow):
        return pltpu.make_async_remote_copy(
            src_ref=src, dst_ref=dst, send_sem=ss, recv_sem=rs,
            device_id={"wide": wide, "narrow": narrow}, device_id_type=MESH)

    def z_copy(c, way, hop, block_z):
        step = 1 - 2 * way
        ref = inv_g.at[block_z * NX + x, pl.ds(c * per, per)]
        return send(ref, ref, zs.at[way, hop], zr.at[c, way, hop], w, (z + step) * NX + x)

    def x_copy(c, block_z, side):
        ref = inv_g.at[block_z * NX + side, pl.ds(c * per, per)]
        return send(ref, ref, xs.at[0], xr.at[c], w, z * NX + 1 - x)

    def can_send(way, hop):
        if way == 0:
            return jnp.logical_and(z - hop >= 0, z + 1 <= nz - 1)
        return jnp.logical_and(z + hop <= nz - 1, z - 1 >= 0)

    def source(way, hop):
        return z - hop if way == 0 else z + hop

    def has_recv(way, hop):
        return z - 1 - hop >= 0 if way == 0 else z + 1 + hop <= nz - 1

    for c in range(CHUNKS):
        for way in range(2):
            @pl.when(can_send(way, 0))
            def _(c=c, way=way):
                z_copy(c, way, 0, source(way, 0)).start()
        x_copy(c, z, x).start()

    loads[1].wait()
    for s in range(nsep):
        def combine(l, carry, s=s):
            acc = jnp.zeros((rows, width), jnp.float32)
            for u in range(nupd):
                pick = jnp.where(tgt_ref[u, l] == s, 1.0, 0.0).astype(jnp.float32)
                acc = acc + pick * upd_ref[l, u].astype(jnp.float32)
            wf[l] = acc
            return carry
        lax.fori_loop(0, leaves, combine, 0)
        wt[pl.ds(s * width, width), :] = wf[...].reshape(leaves * rows, width).T.astype(jnp.bfloat16)

    def relay(c, hop):
        for way in range(2):
            @pl.when(has_recv(way, hop))
            def _(way=way):
                step = 1 - 2 * way
                block_z = source(way, hop + 1)
                ref = inv_g.at[block_z * NX + x, pl.ds(c * per, per)]
                send(ref, ref, zs.at[way, hop], zr.at[c, way, hop], w, (z - step) * NX + x).wait_recv()
                if hop + 1 < nz - 1:
                    @pl.when(can_send(way, hop + 1))
                    def _():
                        z_copy(c, way, hop + 1, block_z).start()
                x_copy(c, block_z, x).start()

    def a_copy(c, peer):
        return send(sol_s.at[peer, pl.ds(c * per, per)], sol_r.at[n, pl.ds(c * per, per)],
                    as_.at[0], ar.at[n], w, peer)

    def group(ref, count, ss, rs):
        part_ref = ref.at[pl.ds(0, count)]
        return send(part_ref, part_ref, ss, rs, w, z * NX + 1 - x)

    def solve(c):
        half = inv_g.at[pl.ds(0, nz), pl.ds(c * per, per)]
        send(half, half, xs.at[0], xr.at[c], w, z * NX + 1 - x).wait_recv()

        def one(i, carry):
            l = c * per + i
            full = inv_g[:, l].reshape(nn * rows, width)
            out = jnp.dot(rhs_ref[l], full, preferred_element_type=jnp.float32)
            sol_ref[l] = out.astype(jnp.bfloat16)
            sol_s[:, l] = out.T.astype(jnp.bfloat16).reshape(nn, rows, scen)
            return carry
        lax.fori_loop(0, per, one, 0)
        for k in range(1, nn):
            a_copy(c, lax.rem(n + k, nn)).start()

    loads[2].wait()
    for wave in range(CHUNKS + nz - 1):
        for hop in range(nz - 1):
            if 0 <= wave - hop < CHUNKS:
                relay(wave - hop, hop)
    for c in range(CHUNKS):
        solve(c)
    sol_r[n] = sol_s[n]

    mate, across = w + 1 - 2 * core, lax.rem(w + 2, 4)

    def pair(k):
        return pl.ds(lax.rem(n + nn - k, nn), 1)

    def c1(k):
        return send(part.at[pair(k), 1 - core], r1.at[pair(k)], s1.at[k], v1.at[k], mate, n)

    def c2(k):
        return send(q1.at[pair(k), 1 - y], r2.at[pair(k)], s2.at[k], v2.at[k], across, n)

    def c3(m):
        return send(q2.at[m], r3.at[n], s3.at[0], v3.at[0], w, m)

    def multiply(k):
        for m in [lax.rem(n + nn - k, nn)]:

            def arrive(m=m):
                send(sol_r.at[m], sol_r.at[m], as_.at[0], ar.at[m], w, z * NX + 1 - x).wait_recv()
            if k:
                arrive()
            block = sol_r[m].reshape(leaves * rows, scen)
            out = jnp.dot(wt[...], block, preferred_element_type=jnp.float32).astype(jnp.bfloat16)
            for a in range(2):
                for b in range(2):
                    q = b * 2 + a
                    part[m, a, b] = out[q * slab:(q + 1) * slab]
        c1(k).start()

    def add_core(k):
        c1(k).wait_recv()
        for m in [lax.rem(n + nn - k, nn)]:
            q1[m] = (part[m, core].astype(jnp.float32) + r1[m].astype(jnp.float32)).astype(jnp.bfloat16)
        c2(k).start()

    def add_across(k):
        c2(k).wait_recv()
        for m in [lax.rem(n + nn - k, nn)]:
            q2[m] = (q1[m, y].astype(jnp.float32) + r2[m].astype(jnp.float32)).astype(jnp.bfloat16)
            if k:
                c3(m).start()

    for i in range(nn + 2):
        if i < nn:
            multiply(i)
        if 0 <= i - 1 < nn:
            add_core(i - 1)
        if 0 <= i - 2 < nn:
            add_across(i - 2)

    total = q2[n].astype(jnp.float32)
    group(r3, nn - 1, s3.at[0], v3.at[0]).wait_recv()
    for k in range(1, nn):
        total = total + r3[lax.rem(n + k, nn)].astype(jnp.float32)
    gall[w] = total.astype(jnp.bfloat16)
    for k in range(1, 4):
        send(gall.at[w], gall.at[w], s4.at[0], v4.at[0], lax.rem(w + k, 4), n).start()
    group(gall, 3, s4.at[0], v4.at[0]).wait_recv()
    gathered = gall[...].astype(jnp.float32).reshape(nsep * width, scen)
    for copy in loads[3:]:
        copy.wait()
    solved = []
    for s in range(nsep):
        reduced = srhs_ref[s].astype(jnp.float32) - gathered[s * width:(s + 1) * width].T
        for t in range(s):
            reduced = reduced - jnp.dot(solved[t], slow_ref[s * (s - 1) // 2 + t], preferred_element_type=jnp.float32)
        solved.append(jnp.dot(reduced.astype(jnp.bfloat16), sinv_ref[s], preferred_element_type=jnp.float32).astype(jnp.bfloat16))
        sep_ref[s] = solved[s]

    for way in range(2):
        for hop in range(nz - 1):
            @pl.when(can_send(way, hop))
            def _(way=way, hop=hop):
                ref = inv_g.at[source(way, hop) * NX + x]
                send(ref, ref, zs.at[way, hop], zr.at[0, way, hop], w, z * NX + 1 - x).wait_send()
    group(inv_g, nz, xs.at[0], xr.at[0]).wait_send()
    group(sol_s, nn - 1, as_.at[0], ar.at[0]).wait_send()
    for k in range(nn):
        c1(k).wait_send()
        c2(k).wait_send()
    group(q2, nn - 1, s3.at[0], v3.at[0]).wait_send()
    group(gall, 3, s4.at[0], v4.at[0]).wait_send()


def fused_body(nn, leaf_rhs, leaf_inv, leaf_upd, leaf_targets, sep_rhs, sep_inv, sep_low):
    leaves, scen, width = leaf_rhs.shape
    rows = leaf_inv.shape[1]
    nsep = sep_inv.shape[0]
    nz = nn // NX
    slab = nsep * width // 4
    bf = jnp.bfloat16
    vmem = pl.BlockSpec(memory_space=pltpu.VMEM)
    hbm = pl.BlockSpec(memory_space=pl.ANY)
    dma = pltpu.SemaphoreType.DMA
    return pl.pallas_call(
        functools.partial(kernel, nz),
        out_shape=(jax.ShapeDtypeStruct(leaf_rhs.shape, bf), jax.ShapeDtypeStruct(sep_rhs.shape, bf)),
        in_specs=[hbm, hbm, hbm, pl.BlockSpec(memory_space=pltpu.SMEM), hbm, hbm, hbm],
        out_specs=(vmem, vmem),
        scratch_shapes=[
            pltpu.VMEM(leaf_rhs.shape, bf), pltpu.VMEM(leaf_upd.shape, bf), pltpu.VMEM(sep_rhs.shape, bf),
            pltpu.VMEM(sep_inv.shape, bf), pltpu.VMEM(sep_low.shape, bf), dma((6,)),
            pltpu.VMEM((nn, leaves, rows, width), bf),
            pltpu.VMEM((nn, leaves, rows, scen), bf),
            pltpu.VMEM((nn, leaves, rows, scen), bf),
            pltpu.VMEM((leaves, rows, width), jnp.float32),
            pltpu.VMEM((nsep * width, leaves * rows), bf),
            pltpu.VMEM((nn, 2, 2, slab, scen), bf),
            pltpu.VMEM((nn, 2, slab, scen), bf),
            pltpu.VMEM((nn, 2, slab, scen), bf),
            pltpu.VMEM((nn, slab, scen), bf),
            pltpu.VMEM((nn, slab, scen), bf),
            pltpu.VMEM((nn, slab, scen), bf),
            pltpu.VMEM((4, slab, scen), bf),
            dma((2, nz)), dma((CHUNKS, 2, nz)),
            dma((1,)), dma((CHUNKS,)),
            dma((1,)), dma((nn,)),
            dma((nn,)), dma((nn,)), dma((nn,)), dma((nn,)), dma((1,)), dma((1,)),
            dma((1,)), dma((1,)),
        ],
        compiler_params=pltpu.CompilerParams(
            collective_id=0, has_side_effects=True, vmem_limit_bytes=56 * 2**20),
    )(leaf_rhs, leaf_inv, leaf_upd, leaf_targets.T, sep_rhs, sep_inv, sep_low)


def solution(mesh):
    if mesh.shape["wide"] == 4 and mesh.shape["narrow"] == 8:
        body = functools.partial(fused_body, mesh.shape["narrow"])
    else:
        body = plain_body
    in_specs = (
        P("wide", "narrow", None),
        P("wide", "narrow", None),
        P("wide", None, "narrow", None),
        P("wide", None),
        P(None, "narrow", None),
        P(),
        P(),
    )
    out_specs = (P("wide", "narrow", None), P(None, "narrow", None))
    return jax.shard_map(body, mesh=mesh, in_specs=in_specs, out_specs=out_specs, check_vma=False)
```

```python
import functools

import jax
import jax.numpy as jnp
from jax import lax
from jax.experimental import pallas as pl
from jax.experimental.pallas import tpu as pltpu
from jax.sharding import PartitionSpec as P


def separator_solve(gathered, sep_rhs, sep_inv, sep_low):
    nsep = sep_inv.shape[0]
    solved_list = []
    for row in range(nsep):
        reduced = sep_rhs[row].astype(jnp.float32) - gathered[row]
        for col in range(row):
            reduced = reduced - jnp.dot(
                solved_list[col],
                sep_low[row * (row - 1) // 2 + col],
                preferred_element_type=jnp.float32,
            )
        reduced = reduced.astype(jnp.bfloat16)
        solved_list.append(
            jnp.dot(reduced, sep_inv[row], preferred_element_type=jnp.float32).astype(jnp.bfloat16)
        )
    return jnp.stack(solved_list)


def plain_body(leaf_rhs, leaf_inv, leaf_upd, leaf_targets, sep_rhs, sep_inv, sep_low):
    nsep = sep_inv.shape[0]
    nupd = leaf_upd.shape[1]
    leaves, scenarios, width = leaf_rhs.shape
    onehot = (leaf_targets[:, :, None] == jnp.arange(nsep, dtype=jnp.int32)[None, None, :]).astype(
        jnp.float32
    )
    columns = leaf_rhs
    leaf_sol = jnp.einsum(
        "lcj,lji->lci",
        columns,
        lax.all_gather(leaf_inv, "narrow", axis=1, tiled=True),
        preferred_element_type=jnp.float32,
    ).astype(jnp.bfloat16)
    start_sum = jnp.zeros((nsep, scenarios, width), jnp.float32)
    total = start_sum
    piece = lax.all_gather(leaf_upd, "narrow", axis=2, tiled=True)
    columns = leaf_sol
    for block in range(nupd):
        contrib = jnp.einsum(
            "lcj,lji->lci", columns, piece[:, block], preferred_element_type=jnp.float32
        )
        total = total + jnp.einsum("lci,ls->sci", contrib, onehot[:, block])
    gathered = total
    total = lax.psum(gathered, "wide")
    sep_sol = separator_solve(total, sep_rhs, sep_inv, sep_low)
    return (leaf_sol, sep_sol)


CHUNKS = 4
NX = 2
MESH = pl.DeviceIdType.MESH


def kernel(nz, rhs_hbm, inv_ref, upd_hbm, tgt_ref, srhs_hbm, sinv_hbm, slow_hbm, sol_ref, sep_ref,
           rhs_ref, upd_ref, srhs_ref, sinv_ref, slow_ref, load, sol_v, store, inv_g, sol_s, sol_r, wf, wt, part, r1, q1, r2, q2, r3, gall,
           zs, zr, xs, xr, as_, ar, s1, v1, s2, v2, s3, v3, s4, v4):
    nn = nz * NX
    w, n = lax.axis_index("wide"), lax.axis_index("narrow")
    core, y = lax.rem(w, 2), w // 2
    z, x = n // NX, lax.rem(n, NX)
    leaves, rows, width = inv_ref.shape
    nupd = upd_hbm.shape[1]
    scen = rhs_hbm.shape[1]
    nsep = sinv_hbm.shape[0]
    per = leaves // CHUNKS
    slab = nsep * width // 4

    loads = [
        pltpu.make_async_copy(src, dst, load.at[i])
        for i, (src, dst) in enumerate([
            (inv_ref, inv_g.at[n]), (upd_hbm, upd_ref), (rhs_hbm, rhs_ref),
            (srhs_hbm, srhs_ref), (sinv_hbm, sinv_ref), (slow_hbm, slow_ref)])
    ]
    loads[0].start()
    barrier = pltpu.get_barrier_semaphore()
    for k in range(1, nn):
        pl.semaphore_signal(barrier, inc=1, device_id={"wide": w, "narrow": lax.rem(n + k, nn)}, device_id_type=MESH)
    for k in range(1, 4):
        pl.semaphore_signal(barrier, inc=1, device_id={"wide": lax.rem(w + k, 4), "narrow": n}, device_id_type=MESH)
    for copy in loads[1:]:
        copy.start()
    loads[0].wait()
    pl.semaphore_wait(barrier, nn - 1 + 3)

    def peer(k):
        zs_of = [z, z + 1 - 2 * lax.rem(z, 2), lax.rem(z + nz // 2, nz), nz - 1 - z]
        return zs_of[k // NX] * NX + (1 - x if k % NX else x)

    def send(src, dst, ss, rs, wide, narrow):
        return pltpu.make_async_remote_copy(
            src_ref=src, dst_ref=dst, send_sem=ss, recv_sem=rs,
            device_id={"wide": wide, "narrow": narrow}, device_id_type=MESH)

    def z_copy(c, way, hop, block_z):
        step = 1 - 2 * way
        ref = inv_g.at[block_z * NX + x, pl.ds(c * per, per)]
        return send(ref, ref, zs.at[way, hop], zr.at[c, way, hop], w, (z + step) * NX + x)

    def x_copy(c, block_z, side):
        ref = inv_g.at[block_z * NX + side, pl.ds(c * per, per)]
        return send(ref, ref, xs.at[0], xr.at[c], w, z * NX + 1 - x)

    def can_send(way, hop):
        if way == 0:
            return jnp.logical_and(z - hop >= 0, z + 1 <= nz - 1)
        return jnp.logical_and(z + hop <= nz - 1, z - 1 >= 0)

    def source(way, hop):
        return z - hop if way == 0 else z + hop

    def has_recv(way, hop):
        return z - 1 - hop >= 0 if way == 0 else z + 1 + hop <= nz - 1

    for c in range(CHUNKS):
        for way in range(2):
            @pl.when(can_send(way, 0))
            def _(c=c, way=way):
                z_copy(c, way, 0, source(way, 0)).start()
        x_copy(c, z, x).start()

    loads[1].wait()
    for s in range(nsep):
        def combine(l, carry, s=s):
            acc = jnp.zeros((rows, width), jnp.float32)
            for u in range(nupd):
                pick = jnp.where(tgt_ref[u, l] == s, 1.0, 0.0).astype(jnp.float32)
                acc = acc + pick * upd_ref[l, u].astype(jnp.float32)
            wf[l] = acc
            return carry
        lax.fori_loop(0, leaves, combine, 0)
        wt[pl.ds(s * width, width), :] = wf[...].reshape(leaves * rows, width).T.astype(jnp.bfloat16)

    def relay(c, hop):
        for way in range(2):
            @pl.when(has_recv(way, hop))
            def _(way=way):
                step = 1 - 2 * way
                block_z = source(way, hop + 1)
                ref = inv_g.at[block_z * NX + x, pl.ds(c * per, per)]
                send(ref, ref, zs.at[way, hop], zr.at[c, way, hop], w, (z - step) * NX + x).wait_recv()
                if hop + 1 < nz - 1:
                    @pl.when(can_send(way, hop + 1))
                    def _():
                        z_copy(c, way, hop + 1, block_z).start()
                x_copy(c, block_z, x).start()

    def a_copy(c, peer):
        return send(sol_s.at[peer, pl.ds(c * per, per)], sol_r.at[n, pl.ds(c * per, per)],
                    as_.at[0], ar.at[n], w, peer)

    def group(ref, count, ss, rs):
        part_ref = ref.at[pl.ds(0, count)]
        return send(part_ref, part_ref, ss, rs, w, z * NX + 1 - x)

    def keep(c):
        piece = pl.ds(c * per, per)
        return pltpu.make_async_copy(sol_v.at[piece], sol_ref.at[piece], store.at[c])

    def solve(c):
        half = inv_g.at[pl.ds(0, nz), pl.ds(c * per, per)]
        send(half, half, xs.at[0], xr.at[c], w, z * NX + 1 - x).wait_recv()

        def one(i, carry):
            l = c * per + i
            full = inv_g[:, l].reshape(nn * rows, width)
            out = jnp.dot(rhs_ref[l], full, preferred_element_type=jnp.float32)
            sol_v[l] = out.astype(jnp.bfloat16)
            sol_s[:, l] = out.T.astype(jnp.bfloat16).reshape(nn, rows, scen)
            return carry
        lax.fori_loop(0, per, one, 0, unroll=True)
        for k in (1, 2, 3, 4, 5, 6, 7):
            a_copy(c, peer(k)).start()
        keep(c).start()

    loads[2].wait()
    for wave in range(CHUNKS + nz - 1):
        for hop in range(nz - 1):
            if 0 <= wave - hop < CHUNKS:
                relay(wave - hop, hop)
    for c in range(CHUNKS):
        solve(c)
    sol_r[n] = sol_s[n]

    mate, across = w + 1 - 2 * core, lax.rem(w + 2, 4)

    def pair(k):
        return pl.ds(peer(k), 1)

    def c1(k):
        return send(part.at[pair(k), 1 - core], r1.at[pair(k)], s1.at[k], v1.at[k], mate, n)

    def c2(k):
        return send(q1.at[pair(k), 1 - y], r2.at[pair(k)], s2.at[k], v2.at[k], across, n)

    def c3(m):
        return send(q2.at[m], r3.at[n], s3.at[0], v3.at[0], w, m)

    def multiply(k):
        for m in [peer(k)]:

            def arrive(m=m):
                send(sol_r.at[m], sol_r.at[m], as_.at[0], ar.at[m], w, z * NX + 1 - x).wait_recv()
            if k:
                arrive()
            block = sol_r[m].reshape(leaves * rows, scen)
            out = jnp.dot(wt[...], block, preferred_element_type=jnp.float32).astype(jnp.bfloat16)
            for a in range(2):
                for b in range(2):
                    q = b * 2 + a
                    part[m, a, b] = out[q * slab:(q + 1) * slab]
        c1(k).start()

    def add_core(k):
        c1(k).wait_recv()
        for m in [peer(k)]:
            q1[m] = (part[m, core].astype(jnp.float32) + r1[m].astype(jnp.float32)).astype(jnp.bfloat16)
        c2(k).start()

    def add_across(k):
        c2(k).wait_recv()
        for m in [peer(k)]:
            q2[m] = (q1[m, y].astype(jnp.float32) + r2[m].astype(jnp.float32)).astype(jnp.bfloat16)
            if k:
                c3(m).start()

    order = (0, 1, 2, 3, 4, 5, 6, 7)
    for i in range(nn + 2):
        if i < nn:
            multiply(order[i])
        if 0 <= i - 1 < nn:
            add_core(order[i - 1])
        if 0 <= i - 2 < nn:
            add_across(order[i - 2])

    total = q2[n].astype(jnp.float32)
    group(r3, nn - 1, s3.at[0], v3.at[0]).wait_recv()
    for k in range(1, nn):
        total = total + r3[lax.rem(n + k, nn)].astype(jnp.float32)
    gall[w] = total.astype(jnp.bfloat16)
    for k in range(1, 4):
        send(gall.at[w], gall.at[w], s4.at[0], v4.at[0], lax.rem(w + k, 4), n).start()
    group(gall, 3, s4.at[0], v4.at[0]).wait_recv()
    gathered = gall[...].astype(jnp.float32).reshape(nsep * width, scen)
    for copy in loads[3:]:
        copy.wait()
    solved = []
    for s in range(nsep):
        reduced = srhs_ref[s].astype(jnp.float32) - gathered[s * width:(s + 1) * width].T
        for t in range(s):
            reduced = reduced - jnp.dot(solved[t], slow_ref[s * (s - 1) // 2 + t], preferred_element_type=jnp.float32)
        solved.append(jnp.dot(reduced.astype(jnp.bfloat16), sinv_ref[s], preferred_element_type=jnp.float32).astype(jnp.bfloat16))
        sep_ref[s] = solved[s]

    for way in range(2):
        for hop in range(nz - 1):
            @pl.when(can_send(way, hop))
            def _(way=way, hop=hop):
                ref = inv_g.at[source(way, hop) * NX + x]
                send(ref, ref, zs.at[way, hop], zr.at[0, way, hop], w, z * NX + 1 - x).wait_send()
    group(inv_g, nz, xs.at[0], xr.at[0]).wait_send()
    for c in range(CHUNKS):
        keep(c).wait()
    group(sol_s, nn - 1, as_.at[0], ar.at[0]).wait_send()
    for k in range(nn):
        c1(k).wait_send()
        c2(k).wait_send()
    group(q2, nn - 1, s3.at[0], v3.at[0]).wait_send()
    group(gall, 3, s4.at[0], v4.at[0]).wait_send()


def fused_body(nn, leaf_rhs, leaf_inv, leaf_upd, leaf_targets, sep_rhs, sep_inv, sep_low):
    leaves, scen, width = leaf_rhs.shape
    rows = leaf_inv.shape[1]
    nsep = sep_inv.shape[0]
    nz = nn // NX
    slab = nsep * width // 4
    bf = jnp.bfloat16
    vmem = pl.BlockSpec(memory_space=pltpu.VMEM)
    hbm = pl.BlockSpec(memory_space=pl.ANY)
    dma = pltpu.SemaphoreType.DMA
    return pl.pallas_call(
        functools.partial(kernel, nz),
        out_shape=(jax.ShapeDtypeStruct(leaf_rhs.shape, bf), jax.ShapeDtypeStruct(sep_rhs.shape, bf)),
        in_specs=[hbm, hbm, hbm, pl.BlockSpec(memory_space=pltpu.SMEM), hbm, hbm, hbm],
        out_specs=(hbm, vmem),
        scratch_shapes=[
            pltpu.VMEM(leaf_rhs.shape, bf), pltpu.VMEM(leaf_upd.shape, bf), pltpu.VMEM(sep_rhs.shape, bf),
            pltpu.VMEM(sep_inv.shape, bf), pltpu.VMEM(sep_low.shape, bf), dma((6,)),
            pltpu.VMEM(leaf_rhs.shape, bf), dma((CHUNKS,)),
            pltpu.VMEM((nn, leaves, rows, width), bf),
            pltpu.VMEM((nn, leaves, rows, scen), bf),
            pltpu.VMEM((nn, leaves, rows, scen), bf),
            pltpu.VMEM((leaves, rows, width), jnp.float32),
            pltpu.VMEM((nsep * width, leaves * rows), bf),
            pltpu.VMEM((nn, 2, 2, slab, scen), bf),
            pltpu.VMEM((nn, 2, slab, scen), bf),
            pltpu.VMEM((nn, 2, slab, scen), bf),
            pltpu.VMEM((nn, slab, scen), bf),
            pltpu.VMEM((nn, slab, scen), bf),
            pltpu.VMEM((nn, slab, scen), bf),
            pltpu.VMEM((4, slab, scen), bf),
            dma((2, nz)), dma((CHUNKS, 2, nz)),
            dma((1,)), dma((CHUNKS,)),
            dma((1,)), dma((nn,)),
            dma((nn,)), dma((nn,)), dma((nn,)), dma((nn,)), dma((1,)), dma((1,)),
            dma((1,)), dma((1,)),
        ],
        compiler_params=pltpu.CompilerParams(
            collective_id=0, has_side_effects=True, vmem_limit_bytes=56 * 2**20),
    )(leaf_rhs, leaf_inv, leaf_upd, leaf_targets.T, sep_rhs, sep_inv, sep_low)


def solution(mesh):
    if mesh.shape["wide"] == 4 and mesh.shape["narrow"] == 8:
        body = functools.partial(fused_body, mesh.shape["narrow"])
    else:
        body = plain_body
    in_specs = (
        P("wide", "narrow", None),
        P("wide", "narrow", None),
        P("wide", None, "narrow", None),
        P("wide", None),
        P(None, "narrow", None),
        P(),
        P(),
    )
    out_specs = (P("wide", "narrow", None), P(None, "narrow", None))
    return jax.shard_map(body, mesh=mesh, in_specs=in_specs, out_specs=out_specs, check_vma=False)
```
